32 devices in a mesh: dp: 2 (over core), space: 16 (over z, y, x).
Axes of the slice: x: 2, y: 2, z: 4, core: 2. Of those that a mesh axis runs over, the one named last changes fastest.
Arguments:
- features: bfloat16 [2, 1024, 16, 1024], P('dp', 'space'), may hold values from -6 to 6
- psi: bfloat16 [2, 1024, 64, 256], P('dp', 'space'), may hold values from -0.75 to 0.75
- neighbors: int32 [2, 1024, 16], P('dp', 'space'), may hold values from 0 to 1023, as said below
- counts: int32 [2, 1024], P('dp', 'space'), may hold values from 4 to 16, as said below
- occupation: float32 [2, 256], P('dp'), may hold values from 0.1 to 1
- weights: bfloat16 [1024, 4096], P(None, 'space'), may hold values from -0.1875 to 0.1875
Outputs:
- energies: float32 [2, 256], P('dp')
- gradient: float32 [4096, 1024], P('space')
The draws below stay inside these ranges and needn't reach their ends.
Inputs may be any that keep to these rules, and one draw needn't show every extreme that they name: `neighbors`: every neighbor tile lies in the same cluster of 64 consecutive tiles or in one of the two clusters beside it, counted around a closed loop of 16 clusters. `counts`: the first tile of every twist uses all 16 slots.
All inputs are finite; a program needn't handle non-finite values.
Results may differ from the reference program's by a relative error of at most 0.004.
Values may be sent and summed in bfloat16 or wider, within the bound.
A program may use at most 192 MiB of HBM per device.

```python
import math
import jax
import jax.numpy as jnp
from jax import lax

ORB = 64
F = 1024
NB = 256
K = 16
TILE_DEV = 64
CLUSTERS = 16
TILES = 1024
TWISTS = 2


def draw_neighbors(key, part):
    first, second = jax.random.split(key)
    base = jnp.arange(TILES, dtype=jnp.int32) // TILE_DEV
    offset = jax.random.randint(first, (TWISTS, TILES, K), -1, 2)
    owner = (base[None, :, None] + offset + CLUSTERS) % CLUSTERS
    return (owner * TILE_DEV + jax.random.randint(second, (TWISTS, TILES, K), 0, TILE_DEV)).astype(jnp.int32)


def draw_counts(key, part):
    drawn = jax.random.randint(key, (TWISTS, TILES), K // 4, K + 1)
    return drawn.at[:, 0].set(K).astype(jnp.int32)


def block_levels(key, extent, cuts, least, largest):
    level, own = 1.0, jax.random.fold_in(key, 6)
    for position, blocks in cuts:
        draws = jnp.exp(jax.random.uniform(jax.random.fold_in(own, position), (blocks,), jnp.float32, least / len(cuts), largest / len(cuts)))
        level = level * jnp.repeat(draws, extent[position] // blocks).reshape([-1 if axis == position else 1 for axis in range(len(extent))])
    return level


def bell_draw(rng, dims, scale, limit, pieces=(), kind=jnp.bfloat16):
    array = scale * jax.random.normal(rng, dims, jnp.float32)
    if pieces:
        array = array * block_levels(rng, dims, pieces, -0.22, 0.18)
    return jnp.clip(array, -limit, limit).astype(kind)


def setup_inputs(seed: int = 0) -> dict:
    arg_keys = jax.random.split(jax.random.key(seed), 7)
    return {
        "features": bell_draw(arg_keys[0], (TWISTS, TILES, K, F), 1.0, 6.0, ((0, 2), (1, 16))),
        "psi": bell_draw(arg_keys[1], (TWISTS, TILES, ORB, NB), 0.125, 0.75, ((0, 2), (1, 16))),
        "neighbors": draw_neighbors(jax.random.fold_in(arg_keys[6], 71), 0),
        "counts": draw_counts(jax.random.fold_in(arg_keys[6], 71), 0),
        "occupation": jnp.clip(jnp.exp(math.log(1.0) - 2.3025851 * jax.random.uniform(arg_keys[4], (TWISTS, NB), jnp.float32) ** block_levels(arg_keys[4], (TWISTS, NB), ((0, 2),), -0.2, 0.2)), 0.1, 1.0),
        "weights": bell_draw(arg_keys[5], (F, ORB * ORB), F ** -0.5, 0.1875, ((1, 16),)),
    }


def reference(features, psi, neighbors, counts, occupation, weights):
    twists, tile_count, slots, width = features.shape
    orbit = psi.shape[2]
    bands = psi.shape[3]
    factor = 1.0 / math.sqrt(tile_count * slots)
    starts = jnp.arange(tile_count // TILE_DEV, dtype=jnp.int32) * TILE_DEV
    gradient = jnp.zeros((orbit * orbit, width), jnp.float32)
    energy_rows = []
    for twist in range(twists):
        table = psi[twist]
        weighted_all = (table.astype(jnp.float32) * occupation[twist][None, None, :]).astype(jnp.bfloat16)
        feats = features[twist]
        nbrs = neighbors[twist]
        cnts = counts[twist]

        def step(carry, start):
            grad_acc, energy = carry
            block_x = lax.dynamic_slice_in_dim(feats, start, TILE_DEV, 0)
            block_n = lax.dynamic_slice_in_dim(nbrs, start, TILE_DEV, 0)
            block_c = lax.dynamic_slice_in_dim(cnts, start, TILE_DEV, 0)
            valid = (lax.broadcasted_iota(jnp.int32, (TILE_DEV, slots), 1) < block_c[:, None]).astype(jnp.bfloat16)
            hblock = jnp.dot(block_x.reshape(TILE_DEV * slots, width), weights, preferred_element_type=jnp.float32)
            hblock = hblock.astype(jnp.bfloat16).reshape(TILE_DEV, slots, orbit, orbit) * valid[:, :, None, None]
            fetched = table[block_n].astype(jnp.float32)
            own = lax.dynamic_slice_in_dim(table, start, TILE_DEV, 0).astype(jnp.float32)
            own_w = lax.dynamic_slice_in_dim(weighted_all, start, TILE_DEV, 0).astype(jnp.float32)
            applied = jnp.einsum('rkac,rkcb->rab', hblock.astype(jnp.float32), fetched)
            energy = energy + factor * lax.optimization_barrier(jnp.sum(own * applied, axis=(0, 1)))
            dblock = (factor * jnp.einsum('rab,rkcb->rkac', own_w, fetched)).astype(jnp.bfloat16)
            dblock = dblock * valid[:, :, None, None]
            grad_acc = grad_acc + jnp.einsum('rko,rkf->of', dblock.reshape(TILE_DEV, slots, orbit * orbit).astype(jnp.float32), block_x.astype(jnp.float32))
            return ((grad_acc, energy), None)
        (gradient, energy), unused = lax.scan(step, (gradient, jnp.zeros((bands,), jnp.float32)), starts)
        energy_rows.append(energy)
    return (jnp.stack(energy_rows, axis=0), gradient)
```

```python
import functools
import math

import jax
import jax.numpy as jnp
from jax import lax
from jax.experimental import pallas as pl
from jax.experimental.pallas import tpu as pltpu
from jax.sharding import PartitionSpec as P

GROUP = 4
PITCH = 40


def with_halo(value, axis, dim):
    size = lax.axis_size(axis)
    up = [(i, (i + 1) % size) for i in range(size)]
    down = [(j, i) for i, j in up]
    before = lax.ppermute(value, axis, up)
    after = lax.ppermute(value, axis, down)
    return jnp.concatenate([before, value, after], axis=dim)


def tile_kernel(
    group, slots, orbit, factor, where_ref, count_ref, h_ref, table_ref, own_ref, occ_ref, d_ref, energy_ref, spread, back, acc
):
    step = pl.program_id(0)
    half = orbit // 2
    lanes = 2 * orbit

    @pl.when(step == 0)
    def _():
        acc[...] = jnp.zeros_like(acc)

    low = lax.broadcasted_iota(jnp.int32, (half, 2 * lanes), 1) % lanes < orbit
    slot = lax.broadcasted_iota(jnp.int32, (slots, 1), 0)
    occ = occ_ref[...]
    total = jnp.zeros(acc.shape, jnp.float32)
    for t in range(group):
        tile = step * group + t
        used = slot < count_ref[tile]
        for q in range(half):
            column = h_ref[t * slots : (t + 1) * slots, q * lanes : (q + 1) * lanes].astype(jnp.float32)
            spread[t, pl.ds(q, slots, stride=PITCH), :] = jnp.where(used, column, 0.0)
        own = own_ref[t * orbit : (t + 1) * orbit, :].astype(jnp.float32)
        weighted = (own * occ).astype(jnp.bfloat16)
        applied = jnp.zeros(acc.shape, jnp.float32)
        for k in range(0, slots, 2):
            block = jnp.concatenate(
                [spread[t, j * PITCH : j * PITCH + half, :] for j in (k, k + 1)], axis=1
            )
            left = jnp.concatenate([jnp.where(low, block, 0.0), jnp.where(low, 0.0, block)], axis=0)
            fetched = [
                table_ref[pl.ds(pl.multiple_of(where_ref[tile * slots + j] * orbit, orbit), orbit), :]
                for j in (k, k + 1)
            ]
            right = jnp.concatenate([fetched[0], fetched[0], fetched[1], fetched[1]], axis=0)
            applied = applied + jnp.dot(left.astype(jnp.bfloat16), right, preferred_element_type=jnp.float32)
            both = lax.dot_general(
                weighted, right, (((1,), (1,)), ((), ())), preferred_element_type=jnp.float32
            )
            chosen = jnp.where(low, both[:half], both[half:]) * factor
            for n, j in enumerate((k, k + 1)):
                back[t, j * PITCH : j * PITCH + half, :] = chosen[:, n * lanes : (n + 1) * lanes]
        total = total + own * applied
        for q in range(half):
            column = back[t, pl.ds(q, slots, stride=PITCH), :]
            d_ref[t * slots : (t + 1) * slots, q * lanes : (q + 1) * lanes] = jnp.where(
                used, column, 0.0
            ).astype(jnp.bfloat16)
    acc[...] += total

    @pl.when(step == pl.num_programs(0) - 1)
    def _():
        energy_ref[...] = factor * jnp.sum(acc[...], axis=0, keepdims=True)


def tiles(blocks, table, own, occupation, where, counts, slots, orbit, factor):
    count = counts.shape[0]
    bands = table.shape[1]
    group = GROUP
    rows, square = blocks.shape
    flops = 2 * rows * square * bands * 4
    return pl.pallas_call(
        functools.partial(tile_kernel, group, slots, orbit, factor),
        out_shape=(
            jax.ShapeDtypeStruct((rows, square), jnp.bfloat16),
            jax.ShapeDtypeStruct((1, bands), jnp.float32),
        ),
        grid_spec=pltpu.PrefetchScalarGridSpec(
            num_scalar_prefetch=2,
            grid=(count // group,),
            in_specs=[
                pl.BlockSpec((group * slots, square), lambda i, *_: (i, 0)),
                pl.BlockSpec(table.shape, lambda i, *_: (0, 0), pipeline_mode=pl.Buffered(1)),
                pl.BlockSpec((group * orbit, bands), lambda i, *_: (i, 0)),
                pl.BlockSpec((1, bands), lambda i, *_: (0, 0)),
            ],
            out_specs=[
                pl.BlockSpec((group * slots, square), lambda i, *_: (i, 0)),
                pl.BlockSpec((1, bands), lambda i, *_: (0, 0)),
            ],
            scratch_shapes=[
                pltpu.VMEM((group, slots * PITCH, 2 * orbit), jnp.float32),
                pltpu.VMEM((group, slots * PITCH, 2 * orbit), jnp.float32),
                pltpu.VMEM((orbit, bands), jnp.float32),
            ],
        ),
        compiler_params=pltpu.CompilerParams(vmem_limit_bytes=40 * 2**20),
        cost_estimate=pl.CostEstimate(flops=flops, bytes_accessed=4 * rows * square, transcendentals=0),
    )(where, counts, blocks, table, own, occupation)


def local(features, psi, neighbors, counts, occupation, weights):
    _, rows, slots, width = features.shape
    orbit, bands = psi.shape[2:]
    nspace = lax.axis_size("space")
    myself = lax.axis_index("space")
    factor = 1.0 / math.sqrt(rows * nspace * slots)
    flat = features.reshape(rows * slots, width)
    own = psi.reshape(rows, orbit // 2, 2, bands).swapaxes(1, 2).reshape(rows * orbit, bands)
    table = with_halo(psi.reshape(rows * orbit, bands), "space", 0)
    where = (neighbors // rows - myself + 1 + nspace) % nspace * rows + neighbors % rows
    blocks = jnp.dot(
        flat, lax.all_gather(weights, "space", axis=1, tiled=True), preferred_element_type=jnp.float32
    ).astype(jnp.bfloat16)
    dblocks, energy = tiles(
        blocks, table, own, occupation, where.reshape(-1), counts.reshape(-1), slots, orbit, factor
    )
    energies = lax.psum(energy, "space")
    partial = lax.dot_general(dblocks, flat, (((0,), (0,)), ((), ())), preferred_element_type=jnp.float32)
    share = lax.psum_scatter(partial, "space", scatter_dimension=0, tiled=True)
    gradient = lax.psum(share, "dp")
    return (energies, gradient)


def solution(mesh):
    placed = (
        P("dp", "space", None, None),
        P("dp", "space", None, None),
        P("dp", "space", None),
        P("dp", "space"),
        P("dp", None),
        P(None, "space"),
    )
    return jax.shard_map(
        local,
        mesh=mesh,
        in_specs=placed,
        out_specs=(P("dp", None), P("space", None)),
        check_vma=False,
    )
```

```python
import functools
import math

import jax
import jax.numpy as jnp
from jax import lax
from jax.experimental import pallas as pl
from jax.experimental.pallas import tpu as pltpu
from jax.sharding import PartitionSpec as P

GROUP = 4
PITCH = 40


def with_halo(value, axis, dim):
    size = lax.axis_size(axis)
    up = [(i, (i + 1) % size) for i in range(size)]
    down = [(j, i) for i, j in up]
    before = lax.ppermute(value, axis, up)
    after = lax.ppermute(value, axis, down)
    return jnp.concatenate([before, value, after], axis=dim)


def swap(value, axis, bit):
    size = lax.axis_size(axis)
    return lax.ppermute(value, axis, [(i, i ^ (1 << bit)) for i in range(size)])


def chains(size):
    bits = list(range(size.bit_length() - 1))
    other = [bit ^ 1 if bit ^ 1 < len(bits) else bit for bit in bits]
    return bits, other


def pair(mine, theirs, mybit, axis):
    return jnp.where(mybit == 0, jnp.stack([mine, theirs], axis), jnp.stack([theirs, mine], axis))


def gather_rows(shard):
    size, me, core = lax.axis_size("space"), lax.axis_index("space"), lax.axis_index("dp")
    rows, width = shard.shape
    halves = lax.dynamic_index_in_dim(shard.reshape(2, 2, rows // 4, width), core, 0, keepdims=False)
    parts = []
    for part, order in enumerate(chains(size)):
        value, done = halves[part], []
        for bit in reversed(order):
            axis = sum(d > bit for d in done)
            value = pair(value, swap(value, "space", bit), me >> bit & 1, axis)
            done.append(bit)
        parts.append(value.reshape(size, rows // 4, width))
    mine = jnp.stack(parts, 1)
    return pair(mine, swap(mine, "dp", 0), core, 1).reshape(size * rows, width)


def scatter_rows(partial):
    size, me, core = lax.axis_size("space"), lax.axis_index("space"), lax.axis_index("dp")
    rows, width = partial.shape[0] // size, partial.shape[1]
    split = partial.reshape(size, 2, 2, rows // 4, width)
    pick = lambda value, where, axis: lax.dynamic_index_in_dim(value, where, axis, keepdims=False)
    parts = []
    for part, order in enumerate(chains(size)):
        piece = split[:, :, part]
        value = pick(piece, core, 1).astype(jnp.float32) + swap(pick(piece, 1 - core, 1), "dp", 0)
        value = value.reshape((2,) * len(order) + value.shape[1:])
        left = sorted(order, reverse=True)
        for bit in order:
            axis, mybit = left.index(bit), me >> bit & 1
            sent = pick(value, 1 - mybit, axis)
            if len(left) > 1:
                sent = sent.astype(jnp.bfloat16)
            value = pick(value, mybit, axis) + swap(sent, "space", bit)
            left.remove(bit)
        parts.append(value)
    mine = jnp.stack(parts)
    return pair(mine, swap(mine, "dp", 0), core, 0).reshape(rows, width)


def tile_kernel(
    group, slots, orbit, factor, where_ref, count_ref, h_ref, table_ref, own_ref, occ_ref, d_ref, energy_ref, spread, back, acc
):
    step = pl.program_id(0)
    half = orbit // 2
    lanes = 2 * orbit

    @pl.when(step == 0)
    def _():
        acc[...] = jnp.zeros_like(acc)

    low = lax.broadcasted_iota(jnp.int32, (half, 2 * lanes), 1) % lanes < orbit
    slot = lax.broadcasted_iota(jnp.int32, (slots, 1), 0)
    occ = occ_ref[...]
    total = jnp.zeros(acc.shape, jnp.float32)
    for t in range(group):
        tile = step * group + t
        used = slot < count_ref[tile]
        for q in range(half):
            column = h_ref[t * slots : (t + 1) * slots, q * lanes : (q + 1) * lanes].astype(jnp.float32)
            spread[t, pl.ds(q, slots, stride=PITCH), :] = jnp.where(used, column, 0.0)
        own = own_ref[t * orbit : (t + 1) * orbit, :].astype(jnp.float32)
        weighted = (own * occ).astype(jnp.bfloat16)
        applied = jnp.zeros(acc.shape, jnp.float32)
        for k in range(0, slots, 2):
            block = jnp.concatenate(
                [spread[t, j * PITCH : j * PITCH + half, :] for j in (k, k + 1)], axis=1
            )
            left = jnp.concatenate([jnp.where(low, block, 0.0), jnp.where(low, 0.0, block)], axis=0)
            fetched = [
                table_ref[pl.ds(pl.multiple_of(where_ref[tile * slots + j] * orbit, orbit), orbit), :]
                for j in (k, k + 1)
            ]
            right = jnp.concatenate([fetched[0], fetched[0], fetched[1], fetched[1]], axis=0)
            applied = applied + jnp.dot(left.astype(jnp.bfloat16), right, preferred_element_type=jnp.float32)
            both = lax.dot_general(
                weighted, right, (((1,), (1,)), ((), ())), preferred_element_type=jnp.float32
            )
            chosen = jnp.where(low, both[:half], both[half:]) * factor
            for n, j in enumerate((k, k + 1)):
                back[t, j * PITCH : j * PITCH + half, :] = chosen[:, n * lanes : (n + 1) * lanes]
        total = total + own * applied
        for q in range(half):
            column = back[t, pl.ds(q, slots, stride=PITCH), :]
            d_ref[t * slots : (t + 1) * slots, q * lanes : (q + 1) * lanes] = jnp.where(
                used, column, 0.0
            ).astype(jnp.bfloat16)
    acc[...] += total

    @pl.when(step == pl.num_programs(0) - 1)
    def _():
        energy_ref[...] = factor * jnp.sum(acc[...], axis=0, keepdims=True)


def tiles(blocks, table, own, occupation, where, counts, slots, orbit, factor):
    count = counts.shape[0]
    bands = table.shape[1]
    group = GROUP
    rows, square = blocks.shape
    flops = 2 * rows * square * bands * 4
    return pl.pallas_call(
        functools.partial(tile_kernel, group, slots, orbit, factor),
        out_shape=(
            jax.ShapeDtypeStruct((rows, square), jnp.bfloat16),
            jax.ShapeDtypeStruct((1, bands), jnp.float32),
        ),
        grid_spec=pltpu.PrefetchScalarGridSpec(
            num_scalar_prefetch=2,
            grid=(count // group,),
            in_specs=[
                pl.BlockSpec((group * slots, square), lambda i, *_: (i, 0)),
                pl.BlockSpec(table.shape, lambda i, *_: (0, 0), pipeline_mode=pl.Buffered(1)),
                pl.BlockSpec((group * orbit, bands), lambda i, *_: (i, 0)),
                pl.BlockSpec((1, bands), lambda i, *_: (0, 0)),
            ],
            out_specs=[
                pl.BlockSpec((group * slots, square), lambda i, *_: (i, 0)),
                pl.BlockSpec((1, bands), lambda i, *_: (0, 0)),
            ],
            scratch_shapes=[
                pltpu.VMEM((group, slots * PITCH, 2 * orbit), jnp.float32),
                pltpu.VMEM((group, slots * PITCH, 2 * orbit), jnp.float32),
                pltpu.VMEM((orbit, bands), jnp.float32),
            ],
        ),
        compiler_params=pltpu.CompilerParams(vmem_limit_bytes=40 * 2**20),
        cost_estimate=pl.CostEstimate(flops=flops, bytes_accessed=4 * rows * square, transcendentals=0),
    )(where, counts, blocks, table, own, occupation)


def local(features, psi, neighbors, counts, occupation, weights):
    _, rows, slots, width = features.shape
    orbit, bands = psi.shape[2:]
    nspace = lax.axis_size("space")
    myself = lax.axis_index("space")
    factor = 1.0 / math.sqrt(rows * nspace * slots)
    flat = features.reshape(rows * slots, width)
    own = psi.reshape(rows, orbit // 2, 2, bands).swapaxes(1, 2).reshape(rows * orbit, bands)
    table = with_halo(psi.reshape(rows * orbit, bands), "space", 0)
    where = (neighbors // rows - myself + 1 + nspace) % nspace * rows + neighbors % rows
    blocks = lax.dot_general(
        flat, gather_rows(weights.T), (((1,), (1,)), ((), ())), preferred_element_type=jnp.float32
    ).astype(jnp.bfloat16)
    dblocks, energy = tiles(
        blocks, table, own, occupation, where.reshape(-1), counts.reshape(-1), slots, orbit, factor
    )
    energies = lax.psum(energy, "space")
    partial = lax.dot_general(dblocks, flat, (((0,), (0,)), ((), ())), preferred_element_type=jnp.float32)
    gradient = scatter_rows(partial.astype(jnp.bfloat16))
    return (energies, gradient)


def solution(mesh):
    placed = (
        P("dp", "space", None, None),
        P("dp", "space", None, None),
        P("dp", "space", None),
        P("dp", "space"),
        P("dp", None),
        P(None, "space"),
    )
    return jax.shard_map(
        local,
        mesh=mesh,
        in_specs=placed,
        out_specs=(P("dp", None), P("space", None)),
        check_vma=False,
    )
```

```python
import functools
import math

import jax
import jax.numpy as jnp
from jax import lax
from jax.experimental import pallas as pl
from jax.experimental.pallas import tpu as pltpu
from jax.sharding import PartitionSpec as P

GROUP = 4
PITCH = 40
PIECES = 4


def halo_pieces(value, axis):
    size = lax.axis_size(axis)
    across = [(i, i ^ 1) for i in range(size)]
    along = [(i, (i + 2 - 4 * (i % 2)) % size) for i in range(size)]
    near = [lax.ppermute(piece, axis, across) for piece in jnp.split(value, PIECES)]
    far = [lax.ppermute(piece, axis, along) for piece in near]
    return near + [value] + far


def swap(value, axis, bit):
    size = lax.axis_size(axis)
    return lax.ppermute(value, axis, [(i, i ^ (1 << bit)) for i in range(size)])


def chains(size):
    bits = list(range(size.bit_length() - 1))
    other = [bit ^ 1 if bit ^ 1 < len(bits) else bit for bit in bits]
    return bits, other


def pair(mine, theirs, mybit, axis):
    return jnp.where(mybit == 0, jnp.stack([mine, theirs], axis), jnp.stack([theirs, mine], axis))


def gather_rows(shard):
    size, me, core = lax.axis_size("space"), lax.axis_index("space"), lax.axis_index("dp")
    rows, width = shard.shape
    halves = lax.dynamic_index_in_dim(shard.reshape(2, 2, rows // 4, width), core, 0, keepdims=False)
    parts = []
    for part, order in enumerate(chains(size)):
        value, done = halves[part], []
        for bit in reversed(order):
            axis = sum(d > bit for d in done)
            value = pair(value, swap(value, "space", bit), me >> bit & 1, axis)
            done.append(bit)
        parts.append(value.reshape(size, rows // 4, width))
    mine = jnp.stack(parts, 1)
    return pair(mine, swap(mine, "dp", 0), core, 1).reshape(size * rows, width)


def scatter_rows(partial):
    size, me, core = lax.axis_size("space"), lax.axis_index("space"), lax.axis_index("dp")
    rows, width = partial.shape[0] // size, partial.shape[1]
    split = partial.reshape(size, 2, 2, rows // 4, width)
    pick = lambda value, where, axis: lax.dynamic_index_in_dim(value, where, axis, keepdims=False)
    parts = []
    for part, order in enumerate(chains(size)):
        piece = split[:, :, part]
        value = pick(piece, core, 1).astype(jnp.float32) + swap(pick(piece, 1 - core, 1), "dp", 0)
        value = value.reshape((2,) * len(order) + value.shape[1:])
        left = sorted(order, reverse=True)
        for bit in order:
            axis, mybit = left.index(bit), me >> bit & 1
            sent = pick(value, 1 - mybit, axis)
            if len(left) > 1:
                sent = sent.astype(jnp.bfloat16)
            value = pick(value, mybit, axis) + swap(sent, "space", bit)
            left.remove(bit)
        parts.append(value)
    mine = jnp.stack(parts)
    return pair(mine, swap(mine, "dp", 0), core, 0).reshape(rows, width)


def tile_kernel(
    group, slots, orbit, factor, where_ref, count_ref, h_ref, own_ref, occ_ref, *rest
):
    *pieces, d_ref, energy_ref, spread, back, acc, table_ref, sems = rest
    step = pl.program_id(0)
    half = orbit // 2
    lanes = 2 * orbit

    @pl.when(step == 0)
    def _():
        acc[...] = jnp.zeros_like(acc)
        copies, at = [], 0
        for n, piece in enumerate(pieces):
            size = piece.shape[0]
            copies.append(pltpu.make_async_copy(piece, table_ref.at[pl.ds(at, size), :], sems.at[n]))
            at += size
        for copy in copies:
            copy.start()
        for copy in copies:
            copy.wait()

    low = lax.broadcasted_iota(jnp.int32, (half, 2 * lanes), 1) % lanes < orbit
    slot = lax.broadcasted_iota(jnp.int32, (slots, 1), 0)
    occ = occ_ref[...]
    total = jnp.zeros(acc.shape, jnp.float32)
    for t in range(group):
        tile = step * group + t
        used = slot < count_ref[tile]
        for q in range(half):
            column = h_ref[t * slots : (t + 1) * slots, q * lanes : (q + 1) * lanes].astype(jnp.float32)
            spread[t, pl.ds(q, slots, stride=PITCH), :] = jnp.where(used, column, 0.0)
        own = own_ref[t * orbit : (t + 1) * orbit, :].astype(jnp.float32)
        weighted = (own * occ).astype(jnp.bfloat16)
        applied = jnp.zeros(acc.shape, jnp.float32)
        for k in range(0, slots, 2):
            block = jnp.concatenate(
                [spread[t, j * PITCH : j * PITCH + half, :] for j in (k, k + 1)], axis=1
            )
            left = jnp.concatenate([jnp.where(low, block, 0.0), jnp.where(low, 0.0, block)], axis=0)
            fetched = [
                table_ref[pl.ds(pl.multiple_of(where_ref[tile * slots + j] * orbit, orbit), orbit), :]
                for j in (k, k + 1)
            ]
            right = jnp.concatenate([fetched[0], fetched[0], fetched[1], fetched[1]], axis=0)
            applied = applied + jnp.dot(left.astype(jnp.bfloat16), right, preferred_element_type=jnp.float32)
            both = lax.dot_general(
                weighted, right, (((1,), (1,)), ((), ())), preferred_element_type=jnp.float32
            )
            chosen = jnp.where(low, both[:half], both[half:]) * factor
            for n, j in enumerate((k, k + 1)):
                back[t, j * PITCH : j * PITCH + half, :] = chosen[:, n * lanes : (n + 1) * lanes]
        total = total + own * applied
        for q in range(half):
            column = back[t, pl.ds(q, slots, stride=PITCH), :]
            d_ref[t * slots : (t + 1) * slots, q * lanes : (q + 1) * lanes] = jnp.where(
                used, column, 0.0
            ).astype(jnp.bfloat16)
    acc[...] += total

    @pl.when(step == pl.num_programs(0) - 1)
    def _():
        energy_ref[...] = factor * jnp.sum(acc[...], axis=0, keepdims=True)


def tiles(blocks, pieces, own, occupation, where, counts, slots, orbit, factor):
    count = counts.shape[0]
    bands = own.shape[1]
    group = GROUP
    rows, square = blocks.shape
    flops = 2 * rows * square * bands * 4
    return pl.pallas_call(
        functools.partial(tile_kernel, group, slots, orbit, factor),
        out_shape=(
            jax.ShapeDtypeStruct((rows, square), jnp.bfloat16),
            jax.ShapeDtypeStruct((1, bands), jnp.float32),
        ),
        grid_spec=pltpu.PrefetchScalarGridSpec(
            num_scalar_prefetch=2,
            grid=(count // group,),
            in_specs=[
                pl.BlockSpec((group * slots, square), lambda i, *_: (i, 0)),
                pl.BlockSpec((group * orbit, bands), lambda i, *_: (i, 0)),
                pl.BlockSpec((1, bands), lambda i, *_: (0, 0)),
                *[pl.BlockSpec(memory_space=pl.ANY) for _ in pieces],
            ],
            out_specs=[
                pl.BlockSpec((group * slots, square), lambda i, *_: (i, 0)),
                pl.BlockSpec((1, bands), lambda i, *_: (0, 0)),
            ],
            scratch_shapes=[
                pltpu.VMEM((group, slots * PITCH, 2 * orbit), jnp.float32),
                pltpu.VMEM((group, slots * PITCH, 2 * orbit), jnp.float32),
                pltpu.VMEM((orbit, bands), jnp.float32),
                pltpu.VMEM((sum(piece.shape[0] for piece in pieces), bands), jnp.bfloat16),
                pltpu.SemaphoreType.DMA((len(pieces),)),
            ],
        ),
        compiler_params=pltpu.CompilerParams(vmem_limit_bytes=40 * 2**20),
        cost_estimate=pl.CostEstimate(flops=flops, bytes_accessed=4 * rows * square, transcendentals=0),
    )(where, counts, blocks, own, occupation, *pieces)


def local(features, psi, neighbors, counts, occupation, weights):
    _, rows, slots, width = features.shape
    orbit, bands = psi.shape[2:]
    nspace = lax.axis_size("space")
    myself = lax.axis_index("space")
    factor = 1.0 / math.sqrt(rows * nspace * slots)
    flat = features.reshape(rows * slots, width)
    own = psi.reshape(rows, orbit // 2, 2, bands).swapaxes(1, 2).reshape(rows * orbit, bands)
    pieces = halo_pieces(psi.reshape(rows * orbit, bands), "space")
    offset = (neighbors // rows - myself + 1 + nspace) % nspace
    offset = jnp.where(myself % 2 == 0, 2 - offset, offset)
    where = offset * rows + neighbors % rows
    blocks = lax.dot_general(
        flat, gather_rows(weights.T), (((1,), (1,)), ((), ())), preferred_element_type=jnp.float32
    ).astype(jnp.bfloat16)
    dblocks, energy = tiles(
        blocks, pieces, own, occupation, where.reshape(-1), counts.reshape(-1), slots, orbit, factor
    )
    energies = energy
    for bit in chains(nspace)[0]:
        energies = energies + swap(energies, "space", bit)
    partial = lax.dot_general(dblocks, flat, (((0,), (0,)), ((), ())), preferred_element_type=jnp.float32)
    gradient = scatter_rows(partial.astype(jnp.bfloat16))
    return (energies, gradient)


def solution(mesh):
    placed = (
        P("dp", "space", None, None),
        P("dp", "space", None, None),
        P("dp", "space", None),
        P("dp", "space"),
        P("dp", None),
        P(None, "space"),
    )
    return jax.shard_map(
        local,
        mesh=mesh,
        in_specs=placed,
        out_specs=(P("dp", None), P("space", None)),
        check_vma=False,
    )
```
